32 devices in a mesh: gx: 8 (over z, y), gy: 4 (over x, core).
Axes of the slice: x: 2, y: 2, z: 4, core: 2. Of those that a mesh axis runs over, the one named last changes fastest.
Arguments:
- positions: float32 [3, 8, 4, 512], P(None, 'gx', 'gy'), may hold values from -0.1 to 255.6, as said below
- species: int32 [8, 4, 512], P('gx', 'gy'), may hold values 0 or 1
- counts: int32 [8, 4], P('gx', 'gy'), may hold values from 16 to 512, as said below
- neighbours: int32 [64, 8, 4, 512], P(None, 'gx', 'gy'), may hold values from 4 to 140, as said below
- embed_weight: bfloat16 [64, 12], replicated, may hold values from -1.75 to 1.75
- mixer_weight: bfloat16 [64, 64], replicated, may hold values from -0.75 to 0.75
- tensor_weight: bfloat16 [32, 64], replicated, may hold values from -0.75 to 0.75
- update_weight: bfloat16 [64, 96], replicated, may hold values from -0.625 to 0.625
- output_weight: float32 [64], replicated, may hold values from -0.75 to 0.75
- pair_scale: float32 [2, 2], replicated, may hold values from 0.1 to 1.9
Outputs:
- atom_energy: float32 [8, 4, 512], P('gx', 'gy')
- forces: float32 [3, 8, 4, 512], P(None, 'gx', 'gy')
The draws below stay inside these ranges and needn't reach their ends.
Inputs may be any that keep to these rules, and one draw needn't show every extreme that they name: `counts`: at least one column holds 512 atoms. `neighbours`: o runs 0..8; t runs -8..7 for the own column (o = 4), -6..6 for the four side columns (o odd), -4..4 for the four diagonal ones; one atom's entries are distinct and never (o, t) = (4, 0). `positions`: x and y lie 0.45 to 4.05 from the corner of a column 4.5 wide; the height of slot s lies within 0.1 of s / 2.
All inputs are finite; a program needn't handle non-finite values. No bound on the sum of `species` on one device may be relied on, other than what follows from the above.
Results may differ from the reference program's by a relative error of at most 0.014.
Values sent between devices are 32-bit elements; how exact they have to be, the bound alone decides.
A program may use at most 128 MiB of HBM per device.

```python
import math
import jax
import jax.numpy as jnp
from jax import lax

NCX = 8
NCY = 4
SLOTS = 512
MAXNB = 64
LATENT = 64
CHANNELS = 16
BASIS = 8


def draw_counts(key, part):
    first, second, third = jax.random.split(key, 3)
    band_start = jax.random.randint(first, (), 0, NCX)
    band_width = max(1, NCX * 5 // 16)
    column_x = jnp.arange(NCX, dtype=jnp.int32)[:, None] * jnp.ones((1, NCY), jnp.int32)
    column_y = jnp.ones((NCX, 1), jnp.int32) * jnp.arange(NCY, dtype=jnp.int32)[None, :]
    inside = jnp.remainder(column_x - band_start, NCX) < band_width
    liquid = jax.random.randint(second, (NCX, NCY), SLOTS * 7 // 8, SLOTS + 1)
    vapour = jax.random.randint(third, (NCX, NCY), 16, max(17, SLOTS // 8))
    filled = jnp.where(inside, liquid, vapour)
    full_one = (column_x == band_start) & (column_y == 0)
    return jnp.where(full_one, SLOTS, filled).astype(jnp.int32)


def draw_neighbours(key, part):
    codes_all = jnp.arange(144, dtype=jnp.int32)
    offset_id = codes_all // 16
    stride = codes_all % 16 - 8
    reach = jnp.where(offset_id == 4, 8, jnp.where(offset_id % 2 == 1, 6, 4))
    allowed = (jnp.abs(stride) <= reach) & (codes_all != 72)
    scores = jax.random.randint(key, (NCX, NCY, SLOTS, 144), 0, 2 ** 20) * 256 + codes_all
    scores = jnp.where(allowed, scores, 2 ** 30)
    picked = lax.top_k(-scores, MAXNB)[1]
    return jnp.transpose(picked, (3, 0, 1, 2)).astype(jnp.int32)


def draw_positions(key, part):
    first, second = jax.random.split(key, 2)
    across = jax.random.uniform(first, (2, NCX, NCY, SLOTS), jnp.float32)
    wobble = jax.random.uniform(second, (1, NCX, NCY, SLOTS), jnp.float32, -1.0, 1.0)
    lateral = 4.5 * (0.1 + 0.8 * across)
    height = 0.5 * jnp.arange(SLOTS, dtype=jnp.float32)[None, None, None, :] + 0.1 * wobble
    return jnp.concatenate([lateral, height], axis=0).astype(jnp.float32)


def plant(result, rng, low, high):
    index_at = [jax.random.randint(jax.random.fold_in(rng, axis), (), 0, length) for axis, length in enumerate(result.shape)]
    widest = result.shape.index(max(result.shape))
    next_to = index_at[:widest] + [(index_at[widest] + 1) % result.shape[widest]] + index_at[widest + 1:]
    return result.at[tuple(index_at)].set(low).at[tuple(next_to)].set(high)


def bell_draw(own_key, extent, scale, limit, kind=jnp.bfloat16):
    array = scale * jax.random.normal(own_key, extent, jnp.float32)
    return jnp.clip(array, min=-limit, max=limit).astype(kind)


def setup_inputs(seed: int = 0) -> dict:
    key_list = jax.random.split(jax.random.key(seed), 11)
    positions = draw_positions(jax.random.fold_in(key_list[10], 71), 0)
    species = plant((jax.random.randint(key_list[1], (NCX, NCY, SLOTS), 0, 3) < 2).astype(jnp.int32), jax.random.fold_in(key_list[1], 1), 0, 1)
    counts = draw_counts(jax.random.fold_in(key_list[10], 71), 0)
    neighbours = draw_neighbours(jax.random.fold_in(key_list[10], 71), 0)
    embed_weight = bell_draw(key_list[4], (LATENT, BASIS + 4), (BASIS + 4) ** -0.5, 1.75)
    mixer_weight = bell_draw(key_list[5], (LATENT, LATENT), LATENT ** -0.5, 0.75)
    tensor_weight = bell_draw(key_list[6], (2 * CHANNELS, LATENT), LATENT ** -0.5, 0.75)
    update_weight = bell_draw(key_list[7], (LATENT, LATENT + 2 * CHANNELS), (LATENT + 2 * CHANNELS) ** -0.5, 0.625)
    output_weight = bell_draw(key_list[8], (LATENT,), LATENT ** -0.5, 0.75, jnp.float32)
    pair_scale = jnp.clip(1.0 + 0.18 * jax.random.normal(key_list[9], (2, 2), jnp.float32), 0.1, 1.9)
    return {"positions": positions, "species": species, "counts": counts, "neighbours": neighbours, "embed_weight": embed_weight, "mixer_weight": mixer_weight, "tensor_weight": tensor_weight, "update_weight": update_weight, "output_weight": output_weight, "pair_scale": pair_scale}


cutoff = 4.5
col_width = 4.5
root_three = math.sqrt(3.0)

def atom_terms(displace, other_kind, centre_kind, centre_live, weights):
    embed_weight, mixer_weight, tensor_weight, update_weight, output_weight, pair_scale = weights
    neigh_count = displace.shape[1]
    row_count = displace.shape[2]
    pair_count = neigh_count * row_count
    basis_count = embed_weight.shape[1] - 4
    channels = tensor_weight.shape[0] // 2
    distance = jnp.sqrt(lax.optimization_barrier(jnp.sum(displace * displace, axis=0)))
    scaled = distance / cutoff
    polynomial = 1.0 - 28.0 * scaled ** 6 + 48.0 * scaled ** 7 - 21.0 * scaled ** 8
    envelope = jnp.where(scaled < 1.0, polynomial, 0.0)
    orders = jnp.arange(1, basis_count + 1, dtype=jnp.float32)[:, None, None]
    bessel = math.sqrt(2.0 / cutoff) * jnp.sin(orders * (math.pi / cutoff) * distance[None]) / distance[None]
    centre_wide = jnp.broadcast_to(centre_kind[None, :], (neigh_count, row_count))
    one_hot = jnp.stack([1.0 - centre_wide, centre_wide, 1.0 - other_kind, other_kind])
    embed_input = jnp.concatenate([bessel, one_hot], axis=0).reshape(basis_count + 4, pair_count).astype(jnp.bfloat16)
    hidden = jax.nn.silu(jnp.dot(embed_weight, embed_input, preferred_element_type=jnp.float32)).astype(jnp.bfloat16)
    latent = (jax.nn.silu(jnp.dot(mixer_weight, hidden, preferred_element_type=jnp.float32)) * envelope.reshape(pair_count)).astype(jnp.bfloat16)
    tensor = jnp.dot(tensor_weight, latent, preferred_element_type=jnp.float32).reshape(2, channels, 1, neigh_count, row_count)
    direction = displace / distance[None]
    harmonics = jnp.concatenate([jnp.ones_like(distance)[None], root_three * direction], axis=0)
    environment = lax.optimization_barrier(jnp.sum(tensor[0] * harmonics[None], axis=2))
    features = tensor[1] * harmonics[None]
    even_part = features[:, 0] * environment[:, 0][:, None, :]
    odd_part = lax.optimization_barrier(jnp.sum(features[:, 1:] * environment[:, 1:][:, :, None, :], axis=1))
    scalars = (0.25 * jnp.concatenate([even_part, odd_part], axis=0)).reshape(2 * channels, pair_count).astype(jnp.bfloat16)
    update_input = jnp.concatenate([latent, scalars], axis=0)
    latent_next = latent.astype(jnp.float32) + jax.nn.silu(jnp.dot(update_weight, update_input, preferred_element_type=jnp.float32))
    pair_energy = jnp.dot(output_weight, latent_next, precision=lax.Precision.HIGHEST).reshape(neigh_count, row_count) * envelope
    species_scale = pair_scale[0, 0] * (1.0 - centre_wide) * (1.0 - other_kind) + pair_scale[0, 1] * (1.0 - centre_wide) * other_kind + pair_scale[1, 0] * centre_wide * (1.0 - other_kind) + pair_scale[1, 1] * centre_wide * other_kind
    return centre_live * lax.optimization_barrier(jnp.sum(species_scale * pair_energy, axis=0))

def column_env(extended, neighbour_codes):
    slots = extended.shape[3]
    flattened = extended.reshape(extended.shape[0], 9 * slots)
    column_live = lax.optimization_barrier(jnp.sum(extended[4], axis=2)).reshape(9)
    offset_id = neighbour_codes // 16
    stride = neighbour_codes % 16 - 8
    selector = (offset_id[None] == jnp.arange(9, dtype=jnp.int32)[:, None, None]).astype(jnp.float32)
    partner_count = lax.optimization_barrier(jnp.sum(selector * column_live[:, None, None], axis=0)).astype(jnp.int32)
    row_ids = jnp.arange(slots, dtype=jnp.int32)[None, :]
    partner_slot = jnp.remainder(row_ids + stride, partner_count)
    flat_index = offset_id * slots + partner_slot
    partner = flattened[:, flat_index]
    centre = extended[:, 1, 1, :]
    shift_x = (offset_id // 3 - 1).astype(jnp.float32) * col_width
    shift_y = (offset_id % 3 - 1).astype(jnp.float32) * col_width
    displace = jnp.stack([partner[0] + shift_x - centre[0][None], partner[1] + shift_y - centre[1][None], partner[2] - centre[2][None]])
    return ((displace, partner[3], centre[3], centre[4]), flat_index)

def run_blocks(surround, first, last, weights):
    displace = surround[0]
    slots = surround[3].shape[0]
    block_width = min(128, slots)

    def advance(block, totals):
        energy_all, grad_all = totals
        row_start = (block * block_width).astype(jnp.int32)
        pieces = [lax.dynamic_slice_in_dim(member, row_start, block_width, axis=member.ndim - 1) for member in surround]

        def energy_of(moved):
            return atom_terms(moved, pieces[1], pieces[2], pieces[3], weights)
        energies, pullback = jax.vjp(energy_of, pieces[0])
        gradient = pullback(jnp.ones_like(energies))[0]
        energy_all = lax.dynamic_update_slice_in_dim(energy_all, energies, row_start, axis=0)
        grad_all = lax.dynamic_update_slice_in_dim(grad_all, gradient, row_start, axis=2)
        return (energy_all, grad_all)
    initial = (jnp.zeros((slots,), jnp.float32), jnp.zeros(displace.shape, jnp.float32))
    return lax.fori_loop(first, last, advance, initial)

def column_forces(gradient, flat_index, slots):
    spread = jnp.zeros((3, 9 * slots), jnp.float32).at[:, flat_index.reshape(-1)].add(-gradient.reshape(3, -1))
    spread = spread.at[:, 4 * slots:5 * slots].add(lax.optimization_barrier(jnp.sum(gradient, axis=1)))
    return spread.reshape(3, 3, 3, slots)

def reference(positions, species, counts, neighbours, embed_weight, mixer_weight, tensor_weight, update_weight, output_weight, pair_scale):
    weights = (embed_weight, mixer_weight, tensor_weight, update_weight, output_weight, pair_scale)
    slot_ids = jnp.arange(SLOTS, dtype=jnp.int32)
    live = (slot_ids[None, None, :] < counts[:, :, None]).astype(jnp.float32)
    stacked = jnp.concatenate([positions, species.astype(jnp.float32)[None], live[None]], axis=0)
    wrapped = jnp.concatenate([stacked[:, -1:], stacked, stacked[:, :1]], axis=1)
    wrapped = jnp.concatenate([wrapped[:, :, -1:], wrapped, wrapped[:, :, :1]], axis=2)
    block_width = min(128, SLOTS)
    offsets = jnp.arange(9, dtype=jnp.int32)
    zero_index = jnp.zeros((), jnp.int32)

    def accumulate(force_total, column):
        column_x = (column // NCY).astype(jnp.int32)
        column_y = (column % NCY).astype(jnp.int32)
        extended = lax.dynamic_slice(wrapped, (zero_index, column_x, column_y, zero_index), (5, 3, 3, SLOTS))
        neighbour_codes = lax.dynamic_slice(neighbours, (zero_index, column_x, column_y, zero_index), (MAXNB, 1, 1, SLOTS)).reshape(MAXNB, SLOTS)
        surround, flat_index = column_env(extended, neighbour_codes)
        own_blocks = (counts[column_x, column_y] + block_width - 1) // block_width
        energy_all, grad_all = run_blocks(surround, jnp.zeros((), jnp.int32), own_blocks.astype(jnp.int32), weights)
        spread = column_forces(grad_all, flat_index, SLOTS)
        target_x = jnp.remainder(column_x + offsets // 3 - 1, NCX)
        target_y = jnp.remainder(column_y + offsets % 3 - 1, NCY)
        targets = ((target_x * NCY + target_y)[:, None] * SLOTS + slot_ids[None, :]).reshape(-1).astype(jnp.int32)
        force_total = force_total.at[:, targets].add(spread.reshape(3, 9 * SLOTS))
        return (force_total, energy_all)
    force_total, energies = lax.scan(accumulate, jnp.zeros((3, NCX * NCY * SLOTS), jnp.float32), jnp.arange(NCX * NCY, dtype=jnp.int32))
    return (energies.reshape(NCX, NCY, SLOTS), force_total.reshape(3, NCX, NCY, SLOTS))
```

```python
import math

import jax
import jax.numpy as jnp
from jax import lax
from jax.experimental import pallas as pl
from jax.experimental.pallas import tpu as pltpu
from jax.sharding import PartitionSpec as P

cutoff = 4.5
col_width = 4.5
root_three = math.sqrt(3.0)
LANES = 128
ROWS = 8
REACH = 8
STRIDES = 16
VMEM_LIMIT = 48 * 1024 * 1024
F32 = jnp.float32
BF16 = jnp.bfloat16


def mm(a, b):
    return jnp.dot(a, b, preferred_element_type=F32)


def wrapped_index(shape, axis, count):
    wide = lax.broadcasted_iota(jnp.int32, shape, axis).astype(F32) - REACH
    turns = jnp.floor((wide + 0.5) / count)
    return wide - turns * count


def split(value, terms):
    pieces = []
    for _ in range(terms):
        piece = value.astype(BF16)
        pieces.append(piece)
        value = value - piece.astype(F32)
    return pieces


def spread_kernel(count_ref, column_ref, wide_ref):
    rows, slots = column_ref.shape
    width = wide_ref.shape[1]
    count = count_ref[0, 0].astype(F32)
    hot = (
        wrapped_index((slots, width), 1, count)
        == lax.broadcasted_iota(jnp.int32, (slots, width), 0).astype(F32)
    )
    table = jnp.where(hot, 1.0, 0.0).astype(BF16)
    high, middle, low = split(column_ref[...], 3)
    wide_ref[...] = (mm(low, table) + mm(middle, table)) + mm(high, table)


def fold_kernel(count_ref, wide_ref, out_ref):
    width = wide_ref.shape[1]
    slots = out_ref.shape[1]
    count = count_ref[0, 0].astype(F32)
    hot = (
        wrapped_index((width, slots), 0, count)
        == lax.broadcasted_iota(jnp.int32, (width, slots), 1).astype(F32)
    )
    table = jnp.where(hot, 1.0, 0.0).astype(BF16)
    high, middle, low = split(wide_ref[...], 3)
    out_ref[...] = (mm(low, table) + mm(middle, table)) + mm(high, table)


def codes_of(index):
    reach = lambda o: 8 if o == 4 else (6 if o % 2 else 4)
    return [o for o in range(9) if abs(index - 8) <= reach(o) and (o, index) != (4, 8)]


def row_of(tile):
    return jnp.concatenate([tile[i : i + 1, :] for i in range(ROWS)], axis=1)


def tile_of(row):
    return jnp.concatenate([row[:, i * LANES : (i + 1) * LANES] for i in range(ROWS)], axis=0)


def lane_sum(value):
    parts = [value[:, i * LANES : (i + 1) * LANES] for i in range(ROWS)]
    while len(parts) > 1:
        parts = [parts[i] + parts[i + 1] for i in range(0, len(parts), 2)]
    return parts[0]


def repeat(value):
    return jnp.concatenate([value] * ROWS, axis=1)


def column_sum(value):
    return jnp.sum(value, axis=0, keepdims=True)


def silu_pair(x):
    sig = 0.5 * jnp.tanh(0.5 * x) + 0.5
    s = x * sig
    return s, sig + s - s * sig


SIN = [(-1) ** i * math.pi ** (2 * i + 1) / math.factorial(2 * i + 1) for i in range(6)]
COS = [(-1) ** i * math.pi ** (2 * i) / math.factorial(2 * i) for i in range(7)]


def poly(x, coefficients):
    total = jnp.full_like(x, coefficients[-1])
    for c in coefficients[-2::-1]:
        total = total * x + c
    return total


DIST, INV, ENV, WEIGHT, SCALE, HX, HY, HZ, OTHER = range(9)
D_ENV, D_DIST, D_HX, D_HY, D_HZ = range(5)


def layer_kernel(
    count_ref,
    scale_ref,
    table_ref,
    own_ref,
    codes_ref,
    embed_ref,
    mixer_ref,
    tensor_ref,
    update_ref,
    embed_t_ref,
    mixer_t_ref,
    tensor_t_ref,
    update_t_ref,
    output_ref,
    energy_ref,
    wide_ref,
    plane,
    dplane,
    bessel_d,
    hidden_d,
    latent,
    mixed,
    mixed_d,
    tensor,
    latent_g,
    feature_g,
    environment,
    environment_g,
    per_stride,
):
    block = pl.program_id(0)
    neigh = codes_ref.shape[0]
    chunks = neigh // ROWS
    span = ROWS * LANES
    width = 2 * LANES

    @pl.when(block == 0)
    def _():
        wide_ref[...] = jnp.zeros_like(wide_ref)
        per_stride[...] = jnp.zeros_like(per_stride)

    start = pl.multiple_of(block * LANES, LANES)
    slab = table_ref[:, pl.ds(start, width)]
    codes = codes_ref[...]

    found = [jnp.zeros((neigh, LANES), F32) for _ in range(4)]
    for index in range(STRIDES):
        turned = slab if index == 0 else pltpu.roll(slab, width - index, 1)
        for o in codes_of(index):
            here = codes == STRIDES * o + index
            for a in range(4):
                row = turned[4 * o + a : 4 * o + a + 1, :LANES]
                found[a] = jnp.where(here, row, found[a])
    own = own_ref[...]
    dx, dy, dz = (found[a] - own[a : a + 1, :] for a in range(3))
    other = found[3]
    kind = own[3:4, :]
    slot = lax.broadcasted_iota(jnp.int32, (1, LANES), 1) + start
    live = jnp.where(slot < count_ref[0, 0], 1.0, 0.0)
    square = dx * dx + dy * dy + dz * dz
    inverse = lax.rsqrt(square)
    distance = square * inverse
    x = distance / cutoff
    x2 = x * x
    x5 = x2 * x2 * x
    x6 = x5 * x
    inside = x < 1.0
    env = jnp.where(inside, 1.0 + x6 * (-28.0 + x * (48.0 - 21.0 * x)), 0.0)
    env_slope = jnp.where(inside, x5 * (-168.0 + x * (336.0 - 168.0 * x)) / cutoff, 0.0)
    scale = live * (
        (1.0 - kind) * (scale_ref[0, 0] * (1.0 - other) + scale_ref[0, 1] * other)
        + kind * (scale_ref[1, 0] * (1.0 - other) + scale_ref[1, 1] * other)
    )
    reach3 = root_three * inverse
    plane[DIST] = jnp.minimum(distance, cutoff)
    plane[INV] = inverse
    plane[ENV] = env
    plane[WEIGHT] = env * scale
    plane[SCALE] = scale
    plane[HX] = dx * reach3
    plane[HY] = dy * reach3
    plane[HZ] = dz * reach3
    plane[OTHER] = other
    environment[...] = jnp.zeros_like(environment)
    environment_g[...] = jnp.zeros_like(environment_g)
    energy_ref[...] = jnp.zeros_like(energy_ref)

    def row(which, c):
        return row_of(plane[which, pl.ds(pl.multiple_of(c * ROWS, ROWS), ROWS), :])

    def put(which, c, value):
        dplane[which, pl.ds(pl.multiple_of(c * ROWS, ROWS), ROWS), :] = tile_of(value)

    order = lax.broadcasted_iota(jnp.int32, (8, span), 0)
    order_f = (order + 1).astype(F32)
    kind_row = repeat(kind)
    norm = math.sqrt(2.0 / cutoff)

    def first(c, carry):
        far, inv, envelope, partner = row(DIST, c), row(INV, c), row(ENV, c), row(OTHER, c)
        turns = order_f * (far * (1.0 / cutoff))
        whole = jnp.floor(turns + 0.5)
        part = turns - whole
        sign = 1.0 - 2.0 * (whole - 2.0 * jnp.floor(0.5 * whole))
        part2 = part * part
        scaled = sign * (norm * inv)
        bessel = scaled * (part * poly(part2, SIN))
        slope = scaled * poly(part2, COS)
        bessel_d[c] = (math.pi / cutoff) * order_f * slope - bessel * inv
        one_hot = jnp.where(
            order == 0,
            1.0 - kind_row,
            jnp.where(
                order == 1,
                kind_row,
                jnp.where(order == 2, 1.0 - partner, jnp.where(order == 3, partner, 0.0)),
            ),
        )
        inputs = jnp.concatenate([bessel, one_hot], axis=0).astype(BF16)
        hidden, slope_h = silu_pair(mm(embed_ref[...], inputs))
        hidden_d[c] = slope_h.astype(BF16)
        active, slope_m = silu_pair(mm(mixer_ref[...], hidden.astype(BF16)))
        mixed[c] = active.astype(BF16)
        mixed_d[c] = (slope_m * envelope).astype(BF16)
        lat = (active * envelope).astype(BF16)
        latent[c] = lat
        t = mm(tensor_ref[...], lat)
        tensor[c] = t
        env_w = t[:16]
        environment[0] += lane_sum(env_w)
        for m, which in enumerate((HX, HY, HZ)):
            environment[m + 1] += lane_sum(env_w * row(which, c))
        return carry

    lax.fori_loop(0, chunks, first, 0)

    def second(c, carry):
        weight = row(WEIGHT, c)
        harm = [row(which, c) for which in (HX, HY, HZ)]
        feat = tensor[c, 16:]
        envs = [repeat(environment[m]) for m in range(4)]
        mixed_env = harm[0] * envs[1] + harm[1] * envs[2] + harm[2] * envs[3]
        lat = latent[c]
        quarter = 0.25 * feat
        scalars = jnp.concatenate([quarter * envs[0], quarter * mixed_env], axis=0).astype(BF16)
        joined = jnp.concatenate([lat, scalars], axis=0)
        s, slope = silu_pair(mm(update_ref[...], joined))
        out = output_ref[...]
        value = column_sum(out * (lat.astype(F32) + s))
        energy_ref[...] += lane_sum(value * weight)
        put(D_ENV, c, value * row(SCALE, c))
        seed = out * weight
        back = mm(update_t_ref[...], (seed * slope).astype(BF16))
        latent_g[c] = (seed + back[:64]).astype(BF16)
        even_g, odd_g = 0.25 * back[64:80], 0.25 * back[80:96]
        feature_g[c] = (even_g * envs[0] + odd_g * mixed_env).astype(BF16)
        environment_g[0] += lane_sum(even_g * feat)
        odd = odd_g * feat
        for m in range(3):
            environment_g[m + 1] += lane_sum(odd * harm[m])
            put(D_HX + m, c, column_sum(odd * envs[m + 1]))
        return carry

    lax.fori_loop(0, chunks, second, 0)

    def third(c, carry):
        harm = [row(which, c) for which in (HX, HY, HZ)]
        grads = [repeat(environment_g[m]) for m in range(4)]
        env_w = tensor[c, :16]
        env_w_g = grads[0] + harm[0] * grads[1] + harm[1] * grads[2] + harm[2] * grads[3]
        tensor_g = jnp.concatenate([env_w_g.astype(BF16), feature_g[c]], axis=0)
        total = latent_g[c].astype(F32) + mm(tensor_t_ref[...], tensor_g)
        at = pl.ds(pl.multiple_of(c * ROWS, ROWS), ROWS)
        dplane[D_ENV, at, :] += tile_of(column_sum(total * mixed[c].astype(F32)))
        mixed_g = (total * mixed_d[c].astype(F32)).astype(BF16)
        hidden_g = mm(mixer_t_ref[...], mixed_g)
        hidden_g = (hidden_g * hidden_d[c].astype(F32)).astype(BF16)
        bessel_g = mm(embed_t_ref[...], hidden_g)[:8]
        put(D_DIST, c, column_sum(bessel_g * bessel_d[c]))
        for m in range(3):
            dplane[D_HX + m, at, :] += tile_of(column_sum(env_w * grads[m + 1]))
        return carry

    lax.fori_loop(0, chunks, third, 0)

    hx, hy, hz = plane[HX], plane[HY], plane[HZ]
    gx, gy, gz = dplane[D_HX], dplane[D_HY], dplane[D_HZ]
    inverse = plane[INV]
    slope = dplane[D_DIST] + dplane[D_ENV] * env_slope
    along = (slope - inverse * (hx * gx + hy * gy + hz * gz)) * (1.0 / root_three)
    side = root_three * inverse
    gradient = [side * gx + along * hx, side * gy + along * hy, side * gz + along * hz]

    for index in range(STRIDES):
        for o in codes_of(index):
            here = codes == STRIDES * o + index
            for a in range(3):
                at = 3 * o + a
                per_stride[index, at : at + 1, :] = -column_sum(jnp.where(here, gradient[a], 0.0))
    for a in range(3):
        per_stride[8, 12 + a : 13 + a, :] = column_sum(gradient[a])
    lines = per_stride.shape[1]
    total = jnp.zeros((lines, width), F32)
    for index in range(STRIDES):
        laid = jnp.concatenate([per_stride[index], jnp.zeros((lines, LANES), F32)], axis=1)
        total = total + (laid if index == 0 else pltpu.roll(laid, index, 1))
    wide_ref[:, pl.ds(start, width)] += total


def shifted(value, axis, by):
    peers = lax.axis_size(axis)
    return lax.ppermute(value, axis, [(i, (i + by) % peers) for i in range(peers)])


def body(
    positions,
    species,
    counts,
    neighbours,
    embed_weight,
    mixer_weight,
    tensor_weight,
    update_weight,
    output_weight,
    pair_scale,
):
    slots = positions.shape[3]
    neigh = neighbours.shape[0]
    width = slots + LANES
    vmem = pl.BlockSpec(memory_space=pltpu.VMEM)
    smem = pl.BlockSpec(memory_space=pltpu.SMEM)
    params = pltpu.CompilerParams(vmem_limit_bytes=VMEM_LIMIT)
    column = jnp.concatenate(
        [positions.reshape(3, slots), species.reshape(1, slots).astype(F32)], axis=0
    )
    wide = pl.pallas_call(
        spread_kernel,
        out_shape=jax.ShapeDtypeStruct((4, width), F32),
        in_specs=[smem, vmem],
        out_specs=vmem,
        compiler_params=params,
    )(counts, column)
    beside = jnp.stack([shifted(wide, "gx", 1), wide, shifted(wide, "gx", -1)])
    around = jnp.stack([shifted(beside, "gy", 1), beside, shifted(beside, "gy", -1)], axis=1)
    steps = jnp.arange(3, dtype=F32) - 1.0
    shift = jnp.stack(
        [
            jnp.broadcast_to(col_width * steps[:, None], (3, 3)),
            jnp.broadcast_to(col_width * steps[None, :], (3, 3)),
            jnp.zeros((3, 3), F32),
            jnp.zeros((3, 3), F32),
        ],
        axis=2,
    )
    table = (around + shift[..., None]).reshape(36, width)

    chunks = neigh // ROWS
    span = ROWS * LANES
    latent = mixer_weight.shape[0]
    embed = jnp.pad(embed_weight, ((0, 0), (0, 4)))
    whole = lambda array: pl.BlockSpec(array.shape, lambda b: (0,) * array.ndim)
    by_block = lambda rows: pl.BlockSpec((rows, LANES), lambda b: (0, b))
    operands = [
        embed,
        mixer_weight,
        tensor_weight,
        update_weight,
        embed.T,
        mixer_weight.T,
        tensor_weight.T,
        update_weight.T,
        output_weight.reshape(latent, 1),
    ]
    energy, partials = pl.pallas_call(
        layer_kernel,
        grid=(slots // LANES,),
        out_shape=(
            jax.ShapeDtypeStruct((1, slots), F32),
            jax.ShapeDtypeStruct((27, width), F32),
        ),
        in_specs=[smem, smem, whole(table), by_block(4), by_block(neigh)]
        + [whole(array) for array in operands],
        out_specs=(by_block(1), pl.BlockSpec((27, width), lambda b: (0, 0))),
        scratch_shapes=[
            pltpu.VMEM((9, neigh, LANES), F32),
            pltpu.VMEM((5, neigh, LANES), F32),
            pltpu.VMEM((chunks, 8, span), F32),
            pltpu.VMEM((chunks, latent, span), BF16),
            pltpu.VMEM((chunks, latent, span), BF16),
            pltpu.VMEM((chunks, latent, span), BF16),
            pltpu.VMEM((chunks, latent, span), BF16),
            pltpu.VMEM((chunks, 32, span), F32),
            pltpu.VMEM((chunks, latent, span), BF16),
            pltpu.VMEM((chunks, 16, span), BF16),
            pltpu.VMEM((4, 16, LANES), F32),
            pltpu.VMEM((4, 16, LANES), F32),
            pltpu.VMEM((STRIDES, 27, LANES), F32),
        ],
        compiler_params=params,
    )(counts, pair_scale, table, column, neighbours.reshape(neigh, slots), *operands)

    partials = partials.reshape(3, 3, 3, width)
    line = partials[1] + shifted(partials[0], "gx", -1) + shifted(partials[2], "gx", 1)
    centre = line[1] + shifted(line[0], "gy", -1) + shifted(line[2], "gy", 1)
    forces = pl.pallas_call(
        fold_kernel,
        out_shape=jax.ShapeDtypeStruct((3, slots), F32),
        in_specs=[smem, vmem],
        out_specs=vmem,
        compiler_params=params,
    )(counts, centre)
    return energy.reshape(1, 1, slots), forces.reshape(3, 1, 1, slots)


def solution(mesh):
    return jax.shard_map(
        body,
        mesh=mesh,
        in_specs=(
            P(None, "gx", "gy", None),
            P("gx", "gy", None),
            P("gx", "gy"),
            P(None, "gx", "gy", None),
            P(),
            P(),
            P(),
            P(),
            P(),
            P(),
        ),
        out_specs=(P("gx", "gy", None), P(None, "gx", "gy", None)),
        check_vma=False,
    )
```

```python
import math

import jax
import jax.numpy as jnp
from jax import lax
from jax.experimental import pallas as pl
from jax.experimental.pallas import tpu as pltpu
from jax.sharding import PartitionSpec as P

cutoff = 4.5
col_width = 4.5
root_three = math.sqrt(3.0)
LANES = 128
ROWS = 8
REACH = 8
STRIDES = 16
VMEM_LIMIT = 48 * 1024 * 1024
F32 = jnp.float32
BF16 = jnp.bfloat16


def mm(a, b):
    return jnp.dot(a, b, preferred_element_type=F32)


def wrapped_index(shape, axis, count):
    wide = lax.broadcasted_iota(jnp.int32, shape, axis).astype(F32) - REACH
    turns = jnp.floor((wide + 0.5) / count)
    return wide - turns * count


def split(value, terms):
    pieces = []
    for _ in range(terms):
        piece = value.astype(BF16)
        pieces.append(piece)
        value = value - piece.astype(F32)
    return pieces


def beside(o):
    gx, gy = lax.axis_size("gx"), lax.axis_size("gy")
    return (
        lax.rem(lax.axis_index("gx") + gx + (o // 3 - 1), gx),
        lax.rem(lax.axis_index("gy") + gy + (o % 3 - 1), gy),
    )


AROUND = (3, 5, 1, 7, 0, 2, 6, 8)
MESH = pl.DeviceIdType.MESH


def greet():
    for o in AROUND:
        pl.semaphore_signal(
            pltpu.get_barrier_semaphore(), inc=1, device_id=beside(o), device_id_type=MESH
        )


def to_column(o, source, held, send_sem, recv_sem):
    return pltpu.make_async_remote_copy(
        src_ref=source,
        dst_ref=held.at[8 - o],
        send_sem=send_sem.at[o],
        recv_sem=recv_sem.at[8 - o],
        device_id=beside(o),
        device_id_type=MESH,
    )


def spread_kernel(count_ref, column_ref, table_ref, wide, held, send_sem, recv_sem):
    greet()
    rows, slots = column_ref.shape
    width = wide.shape[1]
    count = count_ref[0, 0].astype(F32)
    hot = (
        wrapped_index((slots, width), 1, count)
        == lax.broadcasted_iota(jnp.int32, (slots, width), 0).astype(F32)
    )
    hot = jnp.where(hot, 1.0, 0.0).astype(BF16)
    high, middle, low = split(column_ref[...], 3)
    wide[...] = (mm(low, hot) + mm(middle, hot)) + mm(high, hot)
    pl.semaphore_wait(pltpu.get_barrier_semaphore(), len(AROUND))
    copies = [to_column(o, wide, held, send_sem, recv_sem) for o in AROUND]
    for copy in copies:
        copy.start()
    axis = lax.broadcasted_iota(jnp.int32, (4, width), 0)
    table_ref[16:20, :] = wide[...]
    for copy in copies:
        copy.wait()
    for o in AROUND:
        shift = jnp.where(
            axis == 0,
            col_width * (o // 3 - 1),
            jnp.where(axis == 1, col_width * (o % 3 - 1), 0.0),
        )
        table_ref[4 * o : 4 * o + 4, :] = held[o] + shift


def fold_kernel(count_ref, wide_ref, out_ref, sent, held, send_sem, recv_sem):
    greet()
    width = wide_ref.shape[1]
    slots = out_ref.shape[1]
    blank = jnp.zeros((1, width), F32)
    for o in AROUND:
        sent[o] = jnp.concatenate([wide_ref[3 * o : 3 * o + 3, :], blank], axis=0)
    pl.semaphore_wait(pltpu.get_barrier_semaphore(), len(AROUND))
    copies = [to_column(o, sent.at[o], held, send_sem, recv_sem) for o in AROUND]
    for copy in copies:
        copy.start()
    count = count_ref[0, 0].astype(F32)
    hot = (
        wrapped_index((width, slots), 0, count)
        == lax.broadcasted_iota(jnp.int32, (width, slots), 1).astype(F32)
    )
    hot = jnp.where(hot, 1.0, 0.0).astype(BF16)
    total = jnp.concatenate([wide_ref[12:15, :], blank], axis=0)
    for copy in copies:
        copy.wait()
    for o in AROUND:
        total = total + held[o]
    high, middle, low = split(total, 3)
    out_ref[...] = ((mm(low, hot) + mm(middle, hot)) + mm(high, hot))[:3]


def codes_of(index):
    reach = lambda o: 8 if o == 4 else (6 if o % 2 else 4)
    return [o for o in range(9) if abs(index - 8) <= reach(o) and (o, index) != (4, 8)]


def row_of(tile):
    return jnp.concatenate([tile[i : i + 1, :] for i in range(ROWS)], axis=1)


def tile_of(row):
    return jnp.concatenate([row[:, i * LANES : (i + 1) * LANES] for i in range(ROWS)], axis=0)


def lane_sum(value):
    parts = [value[:, i * LANES : (i + 1) * LANES] for i in range(ROWS)]
    while len(parts) > 1:
        parts = [parts[i] + parts[i + 1] for i in range(0, len(parts), 2)]
    return parts[0]


def repeat(value):
    return jnp.concatenate([value] * ROWS, axis=1)


def column_sum(value):
    return jnp.sum(value, axis=0, keepdims=True)


def silu_pair(x):
    sig = 0.5 * jnp.tanh(0.5 * x) + 0.5
    s = x * sig
    return s, sig + s - s * sig


SIN = [(-1) ** i * math.pi ** (2 * i + 1) / math.factorial(2 * i + 1) for i in range(6)]
COS = [(-1) ** i * math.pi ** (2 * i) / math.factorial(2 * i) for i in range(7)]


def poly(x, coefficients):
    total = jnp.full_like(x, coefficients[-1])
    for c in coefficients[-2::-1]:
        total = total * x + c
    return total


DIST, INV, ENV, WEIGHT, SCALE, HX, HY, HZ, OTHER = range(9)
D_ENV, D_DIST, D_HX, D_HY, D_HZ = range(5)


def layer_kernel(
    count_ref,
    scale_ref,
    table_ref,
    own_ref,
    codes_ref,
    embed_ref,
    mixer_ref,
    tensor_ref,
    update_ref,
    embed_t_ref,
    mixer_t_ref,
    tensor_t_ref,
    update_t_ref,
    output_ref,
    energy_ref,
    wide_ref,
    plane,
    dplane,
    bessel_d,
    hidden_d,
    latent,
    mixed,
    mixed_d,
    tensor,
    latent_g,
    feature_g,
    environment,
    environment_g,
    per_stride,
):
    block = pl.program_id(0)
    neigh = codes_ref.shape[0]
    chunks = neigh // ROWS
    span = ROWS * LANES
    width = 2 * LANES

    @pl.when(block == 0)
    def _():
        wide_ref[...] = jnp.zeros_like(wide_ref)
        per_stride[...] = jnp.zeros_like(per_stride)

    start = pl.multiple_of(block * LANES, LANES)
    slab = table_ref[:, pl.ds(start, width)]
    codes = codes_ref[...]

    found = [jnp.zeros((neigh, LANES), F32) for _ in range(4)]
    for index in range(STRIDES):
        turned = slab if index == 0 else pltpu.roll(slab, width - index, 1)
        for o in codes_of(index):
            here = codes == STRIDES * o + index
            for a in range(4):
                row = turned[4 * o + a : 4 * o + a + 1, :LANES]
                found[a] = jnp.where(here, row, found[a])
    own = own_ref[...]
    dx, dy, dz = (found[a] - own[a : a + 1, :] for a in range(3))
    other = found[3]
    kind = own[3:4, :]
    slot = lax.broadcasted_iota(jnp.int32, (1, LANES), 1) + start
    live = jnp.where(slot < count_ref[0, 0], 1.0, 0.0)
    square = dx * dx + dy * dy + dz * dz
    inverse = lax.rsqrt(square)
    distance = square * inverse
    x = distance / cutoff
    x2 = x * x
    x5 = x2 * x2 * x
    x6 = x5 * x
    inside = x < 1.0
    env = jnp.where(inside, 1.0 + x6 * (-28.0 + x * (48.0 - 21.0 * x)), 0.0)
    env_slope = jnp.where(inside, x5 * (-168.0 + x * (336.0 - 168.0 * x)) / cutoff, 0.0)
    scale = live * (
        (1.0 - kind) * (scale_ref[0, 0] * (1.0 - other) + scale_ref[0, 1] * other)
        + kind * (scale_ref[1, 0] * (1.0 - other) + scale_ref[1, 1] * other)
    )
    reach3 = root_three * inverse
    plane[DIST] = jnp.minimum(distance, cutoff)
    plane[INV] = inverse
    plane[ENV] = env
    plane[WEIGHT] = env * scale
    plane[SCALE] = scale
    plane[HX] = dx * reach3
    plane[HY] = dy * reach3
    plane[HZ] = dz * reach3
    plane[OTHER] = other
    environment[...] = jnp.zeros_like(environment)
    environment_g[...] = jnp.zeros_like(environment_g)
    energy_ref[...] = jnp.zeros_like(energy_ref)

    def row(which, c):
        return row_of(plane[which, pl.ds(pl.multiple_of(c * ROWS, ROWS), ROWS), :])

    def put(which, c, value):
        dplane[which, pl.ds(pl.multiple_of(c * ROWS, ROWS), ROWS), :] = tile_of(value)

    order = lax.broadcasted_iota(jnp.int32, (8, span), 0)
    order_f = (order + 1).astype(F32)
    kind_row = repeat(kind)
    norm = math.sqrt(2.0 / cutoff)

    def first(c, carry):
        far, inv, envelope, partner = row(DIST, c), row(INV, c), row(ENV, c), row(OTHER, c)
        turns = order_f * (far * (1.0 / cutoff))
        whole = jnp.floor(turns + 0.5)
        part = turns - whole
        sign = 1.0 - 2.0 * (whole - 2.0 * jnp.floor(0.5 * whole))
        part2 = part * part
        scaled = sign * (norm * inv)
        bessel = scaled * (part * poly(part2, SIN))
        slope = scaled * poly(part2, COS)
        bessel_d[c] = (math.pi / cutoff) * order_f * slope - bessel * inv
        one_hot = jnp.where(
            order == 0,
            1.0 - kind_row,
            jnp.where(
                order == 1,
                kind_row,
                jnp.where(order == 2, 1.0 - partner, jnp.where(order == 3, partner, 0.0)),
            ),
        )
        inputs = jnp.concatenate([bessel, one_hot[:4]], axis=0).astype(BF16)
        hidden, slope_h = silu_pair(mm(embed_ref[...], inputs))
        hidden_d[c] = slope_h.astype(BF16)
        active, slope_m = silu_pair(mm(mixer_ref[...], hidden.astype(BF16)))
        mixed[c] = active.astype(BF16)
        mixed_d[c] = (slope_m * envelope).astype(BF16)
        lat = (active * envelope).astype(BF16)
        latent[c] = lat
        t = mm(tensor_ref[...], lat)
        tensor[c] = t
        env_w = t[:16]
        environment[0] += lane_sum(env_w)
        for m, which in enumerate((HX, HY, HZ)):
            environment[m + 1] += lane_sum(env_w * row(which, c))
        return carry

    lax.fori_loop(0, chunks, first, 0)

    def second(c, carry):
        weight = row(WEIGHT, c)
        harm = [row(which, c) for which in (HX, HY, HZ)]
        feat = tensor[c, 16:]
        envs = [repeat(environment[m]) for m in range(4)]
        mixed_env = harm[0] * envs[1] + harm[1] * envs[2] + harm[2] * envs[3]
        lat = latent[c]
        quarter = 0.25 * feat
        scalars = jnp.concatenate([quarter * envs[0], quarter * mixed_env], axis=0).astype(BF16)
        joined = jnp.concatenate([lat, scalars], axis=0)
        s, slope = silu_pair(mm(update_ref[...], joined))
        out = output_ref[...]
        value = column_sum(out * (lat.astype(F32) + s))
        energy_ref[...] += lane_sum(value * weight)
        put(D_ENV, c, value * row(SCALE, c))
        seed = out * weight
        back = mm(update_t_ref[...], (seed * slope).astype(BF16))
        latent_g[c] = (seed + back[:64]).astype(BF16)
        even_g, odd_g = 0.25 * back[64:80], 0.25 * back[80:96]
        feature_g[c] = (even_g * envs[0] + odd_g * mixed_env).astype(BF16)
        environment_g[0] += lane_sum(even_g * feat)
        odd = odd_g * feat
        for m in range(3):
            environment_g[m + 1] += lane_sum(odd * harm[m])
            put(D_HX + m, c, column_sum(odd * envs[m + 1]))
        return carry

    lax.fori_loop(0, chunks, second, 0)

    def third(c, carry):
        harm = [row(which, c) for which in (HX, HY, HZ)]
        grads = [repeat(environment_g[m]) for m in range(4)]
        env_w = tensor[c, :16]
        env_w_g = grads[0] + harm[0] * grads[1] + harm[1] * grads[2] + harm[2] * grads[3]
        tensor_g = jnp.concatenate([env_w_g.astype(BF16), feature_g[c]], axis=0)
        total = latent_g[c].astype(F32) + mm(tensor_t_ref[...], tensor_g)
        at = pl.ds(pl.multiple_of(c * ROWS, ROWS), ROWS)
        dplane[D_ENV, at, :] += tile_of(column_sum(total * mixed[c].astype(F32)))
        mixed_g = (total * mixed_d[c].astype(F32)).astype(BF16)
        hidden_g = mm(mixer_t_ref[...], mixed_g)
        hidden_g = (hidden_g * hidden_d[c].astype(F32)).astype(BF16)
        bessel_g = mm(embed_t_ref[...], hidden_g)[:8]
        put(D_DIST, c, column_sum(bessel_g * bessel_d[c]))
        for m in range(3):
            dplane[D_HX + m, at, :] += tile_of(column_sum(env_w * grads[m + 1]))
        return carry

    lax.fori_loop(0, chunks, third, 0)

    hx, hy, hz = plane[HX], plane[HY], plane[HZ]
    gx, gy, gz = dplane[D_HX], dplane[D_HY], dplane[D_HZ]
    inverse = plane[INV]
    slope = dplane[D_DIST] + dplane[D_ENV] * env_slope
    along = (slope - inverse * (hx * gx + hy * gy + hz * gz)) * (1.0 / root_three)
    side = root_three * inverse
    gradient = [side * gx + along * hx, side * gy + along * hy, side * gz + along * hz]

    for index in range(STRIDES):
        for o in codes_of(index):
            here = codes == STRIDES * o + index
            for a in range(3):
                at = 3 * o + a
                per_stride[index, at : at + 1, :] = -column_sum(jnp.where(here, gradient[a], 0.0))
    for a in range(3):
        per_stride[8, 12 + a : 13 + a, :] = column_sum(gradient[a])
    lines = per_stride.shape[1]
    total = jnp.zeros((lines, width), F32)
    for index in range(STRIDES):
        laid = jnp.concatenate([per_stride[index], jnp.zeros((lines, LANES), F32)], axis=1)
        total = total + (laid if index == 0 else pltpu.roll(laid, index, 1))
    wide_ref[:, pl.ds(start, width)] += total


def body(
    positions,
    species,
    counts,
    neighbours,
    embed_weight,
    mixer_weight,
    tensor_weight,
    update_weight,
    output_weight,
    pair_scale,
):
    slots = positions.shape[3]
    neigh = neighbours.shape[0]
    width = slots + LANES
    vmem = pl.BlockSpec(memory_space=pltpu.VMEM)
    smem = pl.BlockSpec(memory_space=pltpu.SMEM)
    params = pltpu.CompilerParams(vmem_limit_bytes=VMEM_LIMIT)
    column = jnp.concatenate(
        [positions.reshape(3, slots), species.reshape(1, slots).astype(F32)], axis=0
    )
    sems = [pltpu.SemaphoreType.DMA((9,)), pltpu.SemaphoreType.DMA((9,))]
    table = pl.pallas_call(
        spread_kernel,
        out_shape=jax.ShapeDtypeStruct((36, width), F32),
        in_specs=[smem, vmem],
        out_specs=vmem,
        scratch_shapes=[pltpu.VMEM((4, width), F32), pltpu.VMEM((9, 4, width), F32)] + sems,
        compiler_params=pltpu.CompilerParams(
            vmem_limit_bytes=VMEM_LIMIT, collective_id=0, has_side_effects=True
        ),
    )(counts, column)

    chunks = neigh // ROWS
    span = ROWS * LANES
    latent = mixer_weight.shape[0]
    whole = lambda array: pl.BlockSpec(array.shape, lambda b: (0,) * array.ndim)
    by_block = lambda rows: pl.BlockSpec((rows, LANES), lambda b: (0, b))
    operands = [
        embed_weight,
        mixer_weight,
        tensor_weight,
        update_weight,
        embed_weight.T,
        mixer_weight.T,
        tensor_weight.T,
        update_weight.T,
        output_weight.reshape(latent, 1),
    ]
    energy, partials = pl.pallas_call(
        layer_kernel,
        grid=(slots // LANES,),
        out_shape=(
            jax.ShapeDtypeStruct((1, slots), F32),
            jax.ShapeDtypeStruct((27, width), F32),
        ),
        in_specs=[smem, smem, whole(table), by_block(4), by_block(neigh)]
        + [whole(array) for array in operands],
        out_specs=(by_block(1), pl.BlockSpec((27, width), lambda b: (0, 0))),
        scratch_shapes=[
            pltpu.VMEM((9, neigh, LANES), F32),
            pltpu.VMEM((5, neigh, LANES), F32),
            pltpu.VMEM((chunks, 8, span), F32),
            pltpu.VMEM((chunks, latent, span), BF16),
            pltpu.VMEM((chunks, latent, span), BF16),
            pltpu.VMEM((chunks, latent, span), BF16),
            pltpu.VMEM((chunks, latent, span), BF16),
            pltpu.VMEM((chunks, 32, span), F32),
            pltpu.VMEM((chunks, latent, span), BF16),
            pltpu.VMEM((chunks, 16, span), BF16),
            pltpu.VMEM((4, 16, LANES), F32),
            pltpu.VMEM((4, 16, LANES), F32),
            pltpu.VMEM((STRIDES, 27, LANES), F32),
        ],
        compiler_params=params,
    )(counts, pair_scale, table, column, neighbours.reshape(neigh, slots), *operands)

    forces = pl.pallas_call(
        fold_kernel,
        out_shape=jax.ShapeDtypeStruct((3, slots), F32),
        in_specs=[smem, vmem],
        out_specs=vmem,
        scratch_shapes=[pltpu.VMEM((9, 4, width), F32), pltpu.VMEM((9, 4, width), F32)] + sems,
        compiler_params=pltpu.CompilerParams(
            vmem_limit_bytes=VMEM_LIMIT, collective_id=1, has_side_effects=True
        ),
    )(counts, partials)
    return energy.reshape(1, 1, slots), forces.reshape(3, 1, 1, slots)


def solution(mesh):
    return jax.shard_map(
        body,
        mesh=mesh,
        in_specs=(
            P(None, "gx", "gy", None),
            P("gx", "gy", None),
            P("gx", "gy"),
            P(None, "gx", "gy", None),
            P(),
            P(),
            P(),
            P(),
            P(),
            P(),
        ),
        out_specs=(P("gx", "gy", None), P(None, "gx", "gy", None)),
        check_vma=False,
    )
```

```python
import math

import jax
import jax.numpy as jnp
from jax import lax
from jax.experimental import pallas as pl
from jax.experimental.pallas import tpu as pltpu
from jax.sharding import PartitionSpec as P

cutoff = 4.5
col_width = 4.5
root_three = math.sqrt(3.0)
LANES = 128
ROWS = 8
REACH = 8
STRIDES = 16
VMEM_LIMIT = 48 * 1024 * 1024
F32 = jnp.float32
BF16 = jnp.bfloat16


def mm(a, b):
    return jnp.dot(a, b, preferred_element_type=F32)


def wrapped_index(shape, axis, count):
    wide = lax.broadcasted_iota(jnp.int32, shape, axis).astype(F32) - REACH
    turns = jnp.floor((wide + 0.5) / count)
    return wide - turns * count


def split(value, terms):
    pieces = []
    for _ in range(terms):
        piece = value.astype(BF16)
        pieces.append(piece)
        value = value - piece.astype(F32)
    return pieces


def beside(o):
    gx, gy = lax.axis_size("gx"), lax.axis_size("gy")
    return (
        lax.rem(lax.axis_index("gx") + gx + (o // 3 - 1), gx),
        lax.rem(lax.axis_index("gy") + gy + (o % 3 - 1), gy),
    )


AROUND = (3, 5, 1, 7, 0, 2, 6, 8)
MESH = pl.DeviceIdType.MESH


def greet():
    for o in AROUND:
        pl.semaphore_signal(
            pltpu.get_barrier_semaphore(), inc=1, device_id=beside(o), device_id_type=MESH
        )


def to_column(o, source, held, send_sem, recv_sem):
    return pltpu.make_async_remote_copy(
        src_ref=source,
        dst_ref=held.at[8 - o],
        send_sem=send_sem.at[o],
        recv_sem=recv_sem.at[8 - o],
        device_id=beside(o),
        device_id_type=MESH,
    )


def spread_kernel(count_ref, column_ref, table_ref, wide, held, send_sem, recv_sem):
    greet()
    rows, slots = column_ref.shape
    width = wide.shape[1]
    count = count_ref[0, 0].astype(F32)
    hot = (
        wrapped_index((slots, width), 1, count)
        == lax.broadcasted_iota(jnp.int32, (slots, width), 0).astype(F32)
    )
    hot = jnp.where(hot, 1.0, 0.0).astype(BF16)
    high, middle, low = split(column_ref[...], 3)
    wide[...] = (mm(low, hot) + mm(middle, hot)) + mm(high, hot)
    pl.semaphore_wait(pltpu.get_barrier_semaphore(), len(AROUND))
    copies = [to_column(o, wide, held, send_sem, recv_sem) for o in AROUND]
    for copy in copies:
        copy.start()
    axis = lax.broadcasted_iota(jnp.int32, (4, width), 0)
    table_ref[16:20, :] = wide[...]
    for copy in copies:
        copy.wait()
    for o in AROUND:
        shift = jnp.where(
            axis == 0,
            col_width * (o // 3 - 1),
            jnp.where(axis == 1, col_width * (o % 3 - 1), 0.0),
        )
        table_ref[4 * o : 4 * o + 4, :] = held[o] + shift


def fold_kernel(count_ref, wide_ref, out_ref, sent, held, send_sem, recv_sem):
    greet()
    width = wide_ref.shape[1]
    slots = out_ref.shape[1]
    blank = jnp.zeros((1, width), F32)
    for o in AROUND:
        sent[o] = jnp.concatenate([wide_ref[3 * o : 3 * o + 3, :], blank], axis=0)
    pl.semaphore_wait(pltpu.get_barrier_semaphore(), len(AROUND))
    copies = [to_column(o, sent.at[o], held, send_sem, recv_sem) for o in AROUND]
    for copy in copies:
        copy.start()
    count = count_ref[0, 0].astype(F32)
    hot = (
        wrapped_index((width, slots), 0, count)
        == lax.broadcasted_iota(jnp.int32, (width, slots), 1).astype(F32)
    )
    hot = jnp.where(hot, 1.0, 0.0).astype(BF16)
    total = jnp.concatenate([wide_ref[12:15, :], blank], axis=0)
    for copy in copies:
        copy.wait()
    for o in AROUND:
        total = total + held[o]
    high, middle, low = split(total, 3)
    out_ref[...] = ((mm(low, hot) + mm(middle, hot)) + mm(high, hot))[:3]


def codes_of(index):
    reach = lambda o: 8 if o == 4 else (6 if o % 2 else 4)
    return [o for o in range(9) if abs(index - 8) <= reach(o) and (o, index) != (4, 8)]


def row_of(tile):
    return jnp.concatenate([tile[i : i + 1, :] for i in range(ROWS)], axis=1)


def tile_of(row):
    return jnp.concatenate([row[:, i * LANES : (i + 1) * LANES] for i in range(ROWS)], axis=0)


def lane_sum(value):
    parts = [value[:, i * LANES : (i + 1) * LANES] for i in range(ROWS)]
    while len(parts) > 1:
        parts = [parts[i] + parts[i + 1] for i in range(0, len(parts), 2)]
    return parts[0]


def repeat(value):
    return jnp.concatenate([value] * ROWS, axis=1)


def column_sum(value):
    return jnp.sum(value, axis=0, keepdims=True)


def silu_pair(x):
    x = x.astype(BF16)
    sig = 0.5 * jnp.tanh(0.5 * x) + 0.5
    s = x * sig
    return s, sig + s - s * sig


SIN = [(-1) ** i * math.pi ** (2 * i + 1) / math.factorial(2 * i + 1) for i in range(6)]
COS = [(-1) ** i * math.pi ** (2 * i) / math.factorial(2 * i) for i in range(7)]


def poly(x, coefficients):
    total = jnp.full_like(x, coefficients[-1])
    for c in coefficients[-2::-1]:
        total = total * x + c
    return total


DIST, INV, ENV, WEIGHT, SCALE, HX, HY, HZ, OTHER = range(9)
D_ENV, D_DIST, D_HX, D_HY, D_HZ = range(5)


def layer_kernel(
    count_ref,
    scale_ref,
    table_ref,
    own_ref,
    codes_ref,
    embed_ref,
    mixer_ref,
    tensor_ref,
    update_ref,
    embed_t_ref,
    mixer_t_ref,
    tensor_t_ref,
    update_t_ref,
    output_ref,
    energy_ref,
    wide_ref,
    plane,
    dplane,
    bessel_d,
    hidden_d,
    latent,
    mixed,
    mixed_d,
    tensor,
    latent_g,
    feature_g,
    environment,
    environment_g,
    per_stride,
):
    block = pl.program_id(0)
    neigh = codes_ref.shape[0]
    chunks = neigh // ROWS
    span = ROWS * LANES
    width = 2 * LANES

    @pl.when(block == 0)
    def _():
        wide_ref[...] = jnp.zeros_like(wide_ref)
        per_stride[...] = jnp.zeros_like(per_stride)

    start = pl.multiple_of(block * LANES, LANES)
    slab = table_ref[:, pl.ds(start, width)]
    codes = codes_ref[...]

    found = [jnp.zeros((neigh, LANES), F32) for _ in range(4)]
    for index in range(STRIDES):
        turned = slab if index == 0 else pltpu.roll(slab, width - index, 1)
        for o in codes_of(index):
            here = codes == STRIDES * o + index
            for a in range(4):
                row = turned[4 * o + a : 4 * o + a + 1, :LANES]
                found[a] = jnp.where(here, row, found[a])
    own = own_ref[...]
    dx, dy, dz = (found[a] - own[a : a + 1, :] for a in range(3))
    other = found[3]
    kind = own[3:4, :]
    slot = lax.broadcasted_iota(jnp.int32, (1, LANES), 1) + start
    live = jnp.where(slot < count_ref[0, 0], 1.0, 0.0)
    square = dx * dx + dy * dy + dz * dz
    inverse = lax.rsqrt(square)
    distance = square * inverse
    x = distance / cutoff
    x2 = x * x
    x5 = x2 * x2 * x
    x6 = x5 * x
    inside = x < 1.0
    env = jnp.where(inside, 1.0 + x6 * (-28.0 + x * (48.0 - 21.0 * x)), 0.0)
    env_slope = jnp.where(inside, x5 * (-168.0 + x * (336.0 - 168.0 * x)) / cutoff, 0.0)
    scale = live * (
        (1.0 - kind) * (scale_ref[0, 0] * (1.0 - other) + scale_ref[0, 1] * other)
        + kind * (scale_ref[1, 0] * (1.0 - other) + scale_ref[1, 1] * other)
    )
    reach3 = root_three * inverse
    plane[DIST] = jnp.minimum(distance, cutoff)
    plane[INV] = inverse
    plane[ENV] = env
    plane[WEIGHT] = env * scale
    plane[SCALE] = scale
    plane[HX] = dx * reach3
    plane[HY] = dy * reach3
    plane[HZ] = dz * reach3
    plane[OTHER] = other
    environment[...] = jnp.zeros_like(environment)
    environment_g[...] = jnp.zeros_like(environment_g)
    energy_ref[...] = jnp.zeros_like(energy_ref)

    def row(which, c):
        return row_of(plane[which, pl.ds(pl.multiple_of(c * ROWS, ROWS), ROWS), :])

    def put(which, c, value):
        dplane[which, pl.ds(pl.multiple_of(c * ROWS, ROWS), ROWS), :] = tile_of(value)

    order = lax.broadcasted_iota(jnp.int32, (8, span), 0)
    order_f = (order + 1).astype(F32)
    kind_row = repeat(kind)
    norm = math.sqrt(2.0 / cutoff)

    def first(c, carry):
        far, inv, envelope, partner = row(DIST, c), row(INV, c), row(ENV, c), row(OTHER, c)
        turns = order_f * (far * (1.0 / cutoff))
        whole = jnp.floor(turns + 0.5)
        part = turns - whole
        sign = 1.0 - 2.0 * (whole - 2.0 * jnp.floor(0.5 * whole))
        part2 = part * part
        scaled = sign * (norm * inv)
        bessel = scaled * (part * poly(part2, SIN))
        slope = scaled * poly(part2, COS)
        bessel_d[c] = (math.pi / cutoff) * order_f * slope - bessel * inv
        one_hot = jnp.where(
            order == 0,
            1.0 - kind_row,
            jnp.where(
                order == 1,
                kind_row,
                jnp.where(order == 2, 1.0 - partner, jnp.where(order == 3, partner, 0.0)),
            ),
        )
        inputs = jnp.concatenate([bessel, one_hot[:4]], axis=0).astype(BF16)
        hidden, slope_h = silu_pair(mm(embed_ref[...], inputs))
        hidden_d[c] = slope_h
        active, slope_m = silu_pair(mm(mixer_ref[...], hidden))
        envelope = jnp.broadcast_to(envelope, active.shape).astype(BF16)
        mixed[c] = active
        mixed_d[c] = slope_m * envelope
        lat = active * envelope
        latent[c] = lat
        t = mm(tensor_ref[...], lat)
        tensor[c] = t
        env_w = t[:16]
        environment[0] += lane_sum(env_w)
        for m, which in enumerate((HX, HY, HZ)):
            environment[m + 1] += lane_sum(env_w * row(which, c))
        return carry

    lax.fori_loop(0, chunks, first, 0, unroll=8)

    def second(c, carry):
        weight = row(WEIGHT, c)
        harm = [row(which, c) for which in (HX, HY, HZ)]
        feat = tensor[c, 16:]
        envs = [repeat(environment[m]) for m in range(4)]
        mixed_env = harm[0] * envs[1] + harm[1] * envs[2] + harm[2] * envs[3]
        lat = latent[c]
        quarter = 0.25 * feat
        scalars = jnp.concatenate([quarter * envs[0], quarter * mixed_env], axis=0).astype(BF16)
        joined = jnp.concatenate([lat, scalars], axis=0)
        s, slope = silu_pair(mm(update_ref[...], joined))
        out = output_ref[...]
        value = column_sum(out * (lat.astype(F32) + s.astype(F32)))
        energy_ref[...] += lane_sum(value * weight)
        put(D_ENV, c, value * row(SCALE, c))
        seed = out * weight
        back = mm(update_t_ref[...], seed.astype(BF16) * slope)
        latent_g[c] = (seed + back[:64]).astype(BF16)
        even_g, odd_g = 0.25 * back[64:80], 0.25 * back[80:96]
        feature_g[c] = (even_g * envs[0] + odd_g * mixed_env).astype(BF16)
        environment_g[0] += lane_sum(even_g * feat)
        odd = odd_g * feat
        for m in range(3):
            environment_g[m + 1] += lane_sum(odd * harm[m])
            put(D_HX + m, c, column_sum(odd * envs[m + 1]))
        return carry

    lax.fori_loop(0, chunks, second, 0, unroll=8)

    def third(c, carry):
        harm = [row(which, c) for which in (HX, HY, HZ)]
        grads = [repeat(environment_g[m]) for m in range(4)]
        env_w = tensor[c, :16]
        env_w_g = grads[0] + harm[0] * grads[1] + harm[1] * grads[2] + harm[2] * grads[3]
        tensor_g = jnp.concatenate([env_w_g.astype(BF16), feature_g[c]], axis=0)
        total = latent_g[c].astype(F32) + mm(tensor_t_ref[...], tensor_g)
        at = pl.ds(pl.multiple_of(c * ROWS, ROWS), ROWS)
        dplane[D_ENV, at, :] += tile_of(column_sum(total * mixed[c].astype(F32)))
        mixed_g = total.astype(BF16) * mixed_d[c]
        hidden_g = mm(mixer_t_ref[...], mixed_g)
        hidden_g = hidden_g.astype(BF16) * hidden_d[c]
        bessel_g = mm(embed_t_ref[...], hidden_g)[:8]
        put(D_DIST, c, column_sum(bessel_g * bessel_d[c]))
        for m in range(3):
            dplane[D_HX + m, at, :] += tile_of(column_sum(env_w * grads[m + 1]))
        return carry

    lax.fori_loop(0, chunks, third, 0, unroll=8)

    hx, hy, hz = plane[HX], plane[HY], plane[HZ]
    gx, gy, gz = dplane[D_HX], dplane[D_HY], dplane[D_HZ]
    inverse = plane[INV]
    slope = dplane[D_DIST] + dplane[D_ENV] * env_slope
    along = (slope - inverse * (hx * gx + hy * gy + hz * gz)) * (1.0 / root_three)
    side = root_three * inverse
    gradient = [side * gx + along * hx, side * gy + along * hy, side * gz + along * hz]

    for index in range(STRIDES):
        for o in codes_of(index):
            here = codes == STRIDES * o + index
            for a in range(3):
                at = 3 * o + a
                per_stride[index, at : at + 1, :] = -column_sum(jnp.where(here, gradient[a], 0.0))
    for a in range(3):
        per_stride[8, 12 + a : 13 + a, :] = column_sum(gradient[a])
    lines = per_stride.shape[1]
    total = jnp.zeros((lines, width), F32)
    for index in range(STRIDES):
        laid = jnp.concatenate([per_stride[index], jnp.zeros((lines, LANES), F32)], axis=1)
        total = total + (laid if index == 0 else pltpu.roll(laid, index, 1))
    wide_ref[:, pl.ds(start, width)] += total


def body(
    positions,
    species,
    counts,
    neighbours,
    embed_weight,
    mixer_weight,
    tensor_weight,
    update_weight,
    output_weight,
    pair_scale,
):
    slots = positions.shape[3]
    neigh = neighbours.shape[0]
    width = slots + LANES
    vmem = pl.BlockSpec(memory_space=pltpu.VMEM)
    smem = pl.BlockSpec(memory_space=pltpu.SMEM)
    params = pltpu.CompilerParams(vmem_limit_bytes=VMEM_LIMIT)
    column = jnp.concatenate(
        [positions.reshape(3, slots), species.reshape(1, slots).astype(F32)], axis=0
    )
    sems = [pltpu.SemaphoreType.DMA((9,)), pltpu.SemaphoreType.DMA((9,))]
    table = pl.pallas_call(
        spread_kernel,
        out_shape=jax.ShapeDtypeStruct((36, width), F32),
        in_specs=[smem, vmem],
        out_specs=vmem,
        scratch_shapes=[pltpu.VMEM((4, width), F32), pltpu.VMEM((9, 4, width), F32)] + sems,
        compiler_params=pltpu.CompilerParams(
            vmem_limit_bytes=VMEM_LIMIT, collective_id=0, has_side_effects=True
        ),
    )(counts, column)

    chunks = neigh // ROWS
    span = ROWS * LANES
    latent = mixer_weight.shape[0]
    whole = lambda array: pl.BlockSpec(array.shape, lambda b: (0,) * array.ndim)
    by_block = lambda rows: pl.BlockSpec((rows, LANES), lambda b: (0, b))
    operands = [
        embed_weight,
        mixer_weight,
        tensor_weight,
        update_weight,
        embed_weight.T,
        mixer_weight.T,
        tensor_weight.T,
        update_weight.T,
        output_weight.reshape(latent, 1),
    ]
    energy, partials = pl.pallas_call(
        layer_kernel,
        grid=(slots // LANES,),
        out_shape=(
            jax.ShapeDtypeStruct((1, slots), F32),
            jax.ShapeDtypeStruct((27, width), F32),
        ),
        in_specs=[smem, smem, whole(table), by_block(4), by_block(neigh)]
        + [whole(array) for array in operands],
        out_specs=(by_block(1), pl.BlockSpec((27, width), lambda b: (0, 0))),
        scratch_shapes=[
            pltpu.VMEM((9, neigh, LANES), F32),
            pltpu.VMEM((5, neigh, LANES), F32),
            pltpu.VMEM((chunks, 8, span), F32),
            pltpu.VMEM((chunks, latent, span), BF16),
            pltpu.VMEM((chunks, latent, span), BF16),
            pltpu.VMEM((chunks, latent, span), BF16),
            pltpu.VMEM((chunks, latent, span), BF16),
            pltpu.VMEM((chunks, 32, span), F32),
            pltpu.VMEM((chunks, latent, span), BF16),
            pltpu.VMEM((chunks, 16, span), BF16),
            pltpu.VMEM((4, 16, LANES), F32),
            pltpu.VMEM((4, 16, LANES), F32),
            pltpu.VMEM((STRIDES, 27, LANES), F32),
        ],
        compiler_params=params,
    )(counts, pair_scale, table, column, neighbours.reshape(neigh, slots), *operands)

    forces = pl.pallas_call(
        fold_kernel,
        out_shape=jax.ShapeDtypeStruct((3, slots), F32),
        in_specs=[smem, vmem],
        out_specs=vmem,
        scratch_shapes=[pltpu.VMEM((9, 4, width), F32), pltpu.VMEM((9, 4, width), F32)] + sems,
        compiler_params=pltpu.CompilerParams(
            vmem_limit_bytes=VMEM_LIMIT, collective_id=1, has_side_effects=True
        ),
    )(counts, partials)
    return energy.reshape(1, 1, slots), forces.reshape(3, 1, 1, slots)


def solution(mesh):
    return jax.shard_map(
        body,
        mesh=mesh,
        in_specs=(
            P(None, "gx", "gy", None),
            P("gx", "gy", None),
            P("gx", "gy"),
            P(None, "gx", "gy", None),
            P(),
            P(),
            P(),
            P(),
            P(),
            P(),
        ),
        out_specs=(P("gx", "gy", None), P(None, "gx", "gy", None)),
        check_vma=False,
    )
```

```python
import math

import jax
import jax.numpy as jnp
from jax import lax
from jax.experimental import pallas as pl
from jax.experimental.pallas import tpu as pltpu
from jax.sharding import PartitionSpec as P

cutoff = 4.5
col_width = 4.5
root_three = math.sqrt(3.0)
LANES = 128
ROWS = 8
REACH = 8
STRIDES = 16
VMEM_LIMIT = 48 * 1024 * 1024
F32 = jnp.float32
BF16 = jnp.bfloat16


def mm(a, b):
    return jnp.dot(a, b, preferred_element_type=F32)


def wrapped_index(shape, axis, count):
    wide = lax.broadcasted_iota(jnp.int32, shape, axis).astype(F32) - REACH
    turns = jnp.floor((wide + 0.5) / count)
    return wide - turns * count


def split(value, terms):
    pieces = []
    for _ in range(terms):
        piece = value.astype(BF16)
        pieces.append(piece)
        value = value - piece.astype(F32)
    return pieces


def beside(o):
    gx, gy = lax.axis_size("gx"), lax.axis_size("gy")
    return (
        lax.rem(lax.axis_index("gx") + gx + (o // 3 - 1), gx),
        lax.rem(lax.axis_index("gy") + gy + (o % 3 - 1), gy),
    )


AROUND = (3, 5, 1, 7, 0, 2, 6, 8)
MESH = pl.DeviceIdType.MESH


def greet():
    for o in AROUND:
        pl.semaphore_signal(
            pltpu.get_barrier_semaphore(), inc=1, device_id=beside(o), device_id_type=MESH
        )


def to_column(o, source, held, send_sem, recv_sem):
    return pltpu.make_async_remote_copy(
        src_ref=source,
        dst_ref=held.at[8 - o],
        send_sem=send_sem.at[o],
        recv_sem=recv_sem.at[8 - o],
        device_id=beside(o),
        device_id_type=MESH,
    )


def spread_kernel(count_ref, column_ref, table_ref, wide, held, send_sem, recv_sem):
    greet()
    rows, slots = column_ref.shape
    width = wide.shape[1]
    count = count_ref[0, 0].astype(F32)
    hot = (
        wrapped_index((slots, width), 1, count)
        == lax.broadcasted_iota(jnp.int32, (slots, width), 0).astype(F32)
    )
    hot = jnp.where(hot, 1.0, 0.0).astype(BF16)
    high, middle, low = split(column_ref[...], 3)
    wide[...] = (mm(low, hot) + mm(middle, hot)) + mm(high, hot)
    pl.semaphore_wait(pltpu.get_barrier_semaphore(), len(AROUND))
    copies = [to_column(o, wide, held, send_sem, recv_sem) for o in AROUND]
    for copy in copies:
        copy.start()
    axis = lax.broadcasted_iota(jnp.int32, (4, width), 0)
    table_ref[16:20, :] = wide[...]
    for copy in copies:
        copy.wait()
    for o in AROUND:
        shift = jnp.where(
            axis == 0,
            col_width * (o // 3 - 1),
            jnp.where(axis == 1, col_width * (o % 3 - 1), 0.0),
        )
        table_ref[4 * o : 4 * o + 4, :] = held[o] + shift


def fold_kernel(count_ref, wide_ref, out_ref, sent, held, send_sem, recv_sem):
    greet()
    width = wide_ref.shape[1]
    slots = out_ref.shape[1]
    blank = jnp.zeros((1, width), F32)
    for o in AROUND:
        sent[o] = jnp.concatenate([wide_ref[3 * o : 3 * o + 3, :], blank], axis=0)
    pl.semaphore_wait(pltpu.get_barrier_semaphore(), len(AROUND))
    copies = [to_column(o, sent.at[o], held, send_sem, recv_sem) for o in AROUND]
    for copy in copies:
        copy.start()
    count = count_ref[0, 0].astype(F32)
    hot = (
        wrapped_index((width, slots), 0, count)
        == lax.broadcasted_iota(jnp.int32, (width, slots), 1).astype(F32)
    )
    hot = jnp.where(hot, 1.0, 0.0).astype(BF16)
    total = jnp.concatenate([wide_ref[12:15, :], blank], axis=0)
    for copy in copies:
        copy.wait()
    for o in AROUND:
        total = total + held[o]
    high, middle, low = split(total, 3)
    out_ref[...] = ((mm(low, hot) + mm(middle, hot)) + mm(high, hot))[:3]


def codes_of(index):
    reach = lambda o: 8 if o == 4 else (6 if o % 2 else 4)
    return [o for o in range(9) if abs(index - 8) <= reach(o) and (o, index) != (4, 8)]


def row_of(tile):
    return jnp.concatenate([tile[i : i + 1, :] for i in range(ROWS)], axis=1)


def tile_of(row):
    return jnp.concatenate([row[:, i * LANES : (i + 1) * LANES] for i in range(ROWS)], axis=0)


def lane_sum(value):
    parts = [value[:, i * LANES : (i + 1) * LANES] for i in range(ROWS)]
    while len(parts) > 1:
        parts = [parts[i] + parts[i + 1] for i in range(0, len(parts), 2)]
    return parts[0]


def repeat(value):
    return jnp.concatenate([value] * ROWS, axis=1)


def column_sum(value):
    return jnp.sum(value, axis=0, keepdims=True)


def silu_pair(x):
    x = x.astype(BF16)
    sig = 0.5 * jnp.tanh(0.5 * x) + 0.5
    s = x * sig
    return s, sig + s - s * sig


SIN = [(-1) ** i * math.pi ** (2 * i + 1) / math.factorial(2 * i + 1) for i in range(6)]
COS = [(-1) ** i * math.pi ** (2 * i) / math.factorial(2 * i) for i in range(7)]


def poly(x, coefficients):
    total = jnp.full_like(x, coefficients[-1])
    for c in coefficients[-2::-1]:
        total = total * x + c
    return total


DIST, INV, ENV, WEIGHT, SCALE, HX, HY, HZ, OTHER = range(9)
D_ENV, D_DIST, D_HX, D_HY, D_HZ = range(5)


def layer_kernel(
    count_ref,
    scale_ref,
    table_ref,
    own_ref,
    codes_ref,
    embed_t_ref,
    mixer_ref,
    tensor_ref,
    update_ref,
    output_ref,
    energy_ref,
    wide_ref,
    plane,
    dplane,
    bessel_d,
    hidden_d,
    latent,
    mixed,
    mixed_d,
    tensor,
    latent_g,
    feature_g,
    environment,
    environment_g,
    per_stride,
    embed_ref,
    mixer_t_ref,
    tensor_t_ref,
    update_t_ref,
):
    block = pl.program_id(0)
    neigh = codes_ref.shape[0]
    chunks = neigh // ROWS
    span = ROWS * LANES
    width = 2 * LANES

    @pl.when(block == 0)
    def _():
        wide_ref[...] = jnp.zeros_like(wide_ref)
        per_stride[...] = jnp.zeros_like(per_stride)
        embed_ref[...] = embed_t_ref[...].astype(F32).T.astype(BF16)
        mixer_t_ref[...] = mixer_ref[...].astype(F32).T.astype(BF16)
        tensor_t_ref[...] = tensor_ref[...].astype(F32).T.astype(BF16)
        update_t_ref[...] = update_ref[...].astype(F32).T.astype(BF16)

    start = pl.multiple_of(block * LANES, LANES)
    slab = table_ref[:, pl.ds(start, width)]
    codes = codes_ref[...]

    found = [jnp.zeros((neigh, LANES), F32) for _ in range(4)]
    for index in range(STRIDES):
        turned = slab if index == 0 else pltpu.roll(slab, width - index, 1)
        for o in codes_of(index):
            here = codes == STRIDES * o + index
            for a in range(4):
                row = turned[4 * o + a : 4 * o + a + 1, :LANES]
                found[a] = jnp.where(here, row, found[a])
    own = own_ref[...]
    dx, dy, dz = (found[a] - own[a : a + 1, :] for a in range(3))
    other = found[3]
    kind = own[3:4, :]
    slot = lax.broadcasted_iota(jnp.int32, (1, LANES), 1) + start
    live = jnp.where(slot < count_ref[0, 0], 1.0, 0.0)
    square = dx * dx + dy * dy + dz * dz
    inverse = lax.rsqrt(square)
    distance = square * inverse
    x = distance / cutoff
    x2 = x * x
    x5 = x2 * x2 * x
    x6 = x5 * x
    inside = x < 1.0
    env = jnp.where(inside, 1.0 + x6 * (-28.0 + x * (48.0 - 21.0 * x)), 0.0)
    env_slope = jnp.where(inside, x5 * (-168.0 + x * (336.0 - 168.0 * x)) / cutoff, 0.0)
    scale = live * (
        (1.0 - kind) * (scale_ref[0, 0] * (1.0 - other) + scale_ref[0, 1] * other)
        + kind * (scale_ref[1, 0] * (1.0 - other) + scale_ref[1, 1] * other)
    )
    reach3 = root_three * inverse
    plane[DIST] = jnp.minimum(distance, cutoff)
    plane[INV] = inverse
    plane[ENV] = env
    plane[WEIGHT] = env * scale
    plane[SCALE] = scale
    plane[HX] = dx * reach3
    plane[HY] = dy * reach3
    plane[HZ] = dz * reach3
    plane[OTHER] = other
    environment[...] = jnp.zeros_like(environment)
    environment_g[...] = jnp.zeros_like(environment_g)
    energy_ref[...] = jnp.zeros_like(energy_ref)

    def row(which, c):
        return row_of(plane[which, pl.ds(pl.multiple_of(c * ROWS, ROWS), ROWS), :])

    def put(which, c, value):
        dplane[which, pl.ds(pl.multiple_of(c * ROWS, ROWS), ROWS), :] = tile_of(value)

    order = lax.broadcasted_iota(jnp.int32, (8, span), 0)
    order_f = (order + 1).astype(F32)
    kind_row = repeat(kind)
    norm = math.sqrt(2.0 / cutoff)

    def first(c, carry):
        far, inv, envelope, partner = row(DIST, c), row(INV, c), row(ENV, c), row(OTHER, c)
        turns = order_f * (far * (1.0 / cutoff))
        whole = jnp.floor(turns + 0.5)
        part = turns - whole
        sign = 1.0 - 2.0 * (whole - 2.0 * jnp.floor(0.5 * whole))
        part2 = part * part
        scaled = sign * (norm * inv)
        bessel = scaled * (part * poly(part2, SIN))
        slope = scaled * poly(part2, COS)
        bessel_d[c] = (math.pi / cutoff) * order_f * slope - bessel * inv
        one_hot = jnp.where(
            order == 0,
            1.0 - kind_row,
            jnp.where(
                order == 1,
                kind_row,
                jnp.where(order == 2, 1.0 - partner, jnp.where(order == 3, partner, 0.0)),
            ),
        )
        inputs = jnp.concatenate([bessel, one_hot[:4]], axis=0).astype(BF16)
        hidden, slope_h = silu_pair(mm(embed_ref[...], inputs))
        hidden_d[c] = slope_h
        active, slope_m = silu_pair(mm(mixer_ref[...], hidden))
        envelope = jnp.broadcast_to(envelope, active.shape).astype(BF16)
        mixed[c] = active
        mixed_d[c] = slope_m * envelope
        lat = active * envelope
        latent[c] = lat
        t = mm(tensor_ref[...], lat)
        tensor[c] = t
        env_w = t[:16]
        environment[0] += lane_sum(env_w)
        for m, which in enumerate((HX, HY, HZ)):
            environment[m + 1] += lane_sum(env_w * row(which, c))
        return carry

    lax.fori_loop(0, chunks, first, 0, unroll=8)

    def second(c, carry):
        weight = row(WEIGHT, c)
        harm = [row(which, c) for which in (HX, HY, HZ)]
        feat = tensor[c, 16:]
        envs = [repeat(environment[m]) for m in range(4)]
        mixed_env = harm[0] * envs[1] + harm[1] * envs[2] + harm[2] * envs[3]
        lat = latent[c]
        quarter = 0.25 * feat
        scalars = jnp.concatenate([quarter * envs[0], quarter * mixed_env], axis=0).astype(BF16)
        joined = jnp.concatenate([lat, scalars], axis=0)
        s, slope = silu_pair(mm(update_ref[...], joined))
        out = output_ref[...]
        value = column_sum(out * (lat.astype(F32) + s.astype(F32)))
        energy_ref[...] += lane_sum(value * weight)
        put(D_ENV, c, value * row(SCALE, c))
        seed = out * weight
        back = mm(update_t_ref[...], seed.astype(BF16) * slope)
        latent_g[c] = (seed + back[:64]).astype(BF16)
        even_g, odd_g = 0.25 * back[64:80], 0.25 * back[80:96]
        feature_g[c] = (even_g * envs[0] + odd_g * mixed_env).astype(BF16)
        environment_g[0] += lane_sum(even_g * feat)
        odd = odd_g * feat
        for m in range(3):
            environment_g[m + 1] += lane_sum(odd * harm[m])
            put(D_HX + m, c, column_sum(odd * envs[m + 1]))
        return carry

    lax.fori_loop(0, chunks, second, 0, unroll=8)

    def third(c, carry):
        harm = [row(which, c) for which in (HX, HY, HZ)]
        grads = [repeat(environment_g[m]) for m in range(4)]
        env_w = tensor[c, :16]
        env_w_g = grads[0] + harm[0] * grads[1] + harm[1] * grads[2] + harm[2] * grads[3]
        tensor_g = jnp.concatenate([env_w_g.astype(BF16), feature_g[c]], axis=0)
        total = latent_g[c].astype(F32) + mm(tensor_t_ref[...], tensor_g)
        at = pl.ds(pl.multiple_of(c * ROWS, ROWS), ROWS)
        dplane[D_ENV, at, :] += tile_of(column_sum(total * mixed[c].astype(F32)))
        mixed_g = total.astype(BF16) * mixed_d[c]
        hidden_g = mm(mixer_t_ref[...], mixed_g)
        hidden_g = hidden_g.astype(BF16) * hidden_d[c]
        bessel_g = mm(embed_t_ref[...], hidden_g)[:8]
        put(D_DIST, c, column_sum(bessel_g * bessel_d[c]))
        for m in range(3):
            dplane[D_HX + m, at, :] += tile_of(column_sum(env_w * grads[m + 1]))
        return carry

    lax.fori_loop(0, chunks, third, 0, unroll=8)

    hx, hy, hz = plane[HX], plane[HY], plane[HZ]
    gx, gy, gz = dplane[D_HX], dplane[D_HY], dplane[D_HZ]
    inverse = plane[INV]
    slope = dplane[D_DIST] + dplane[D_ENV] * env_slope
    along = (slope - inverse * (hx * gx + hy * gy + hz * gz)) * (1.0 / root_three)
    side = root_three * inverse
    gradient = [side * gx + along * hx, side * gy + along * hy, side * gz + along * hz]

    for index in range(STRIDES):
        for o in codes_of(index):
            here = codes == STRIDES * o + index
            for a in range(3):
                at = 3 * o + a
                per_stride[index, at : at + 1, :] = -column_sum(jnp.where(here, gradient[a], 0.0))
    for a in range(3):
        per_stride[8, 12 + a : 13 + a, :] = column_sum(gradient[a])
    lines = per_stride.shape[1]
    total = jnp.zeros((lines, width), F32)
    for index in range(STRIDES):
        laid = jnp.concatenate([per_stride[index], jnp.zeros((lines, LANES), F32)], axis=1)
        total = total + (laid if index == 0 else pltpu.roll(laid, index, 1))
    wide_ref[:, pl.ds(start, width)] += total


def body(
    positions,
    species,
    counts,
    neighbours,
    embed_weight,
    mixer_weight,
    tensor_weight,
    update_weight,
    output_weight,
    pair_scale,
):
    slots = positions.shape[3]
    neigh = neighbours.shape[0]
    width = slots + LANES
    vmem = pl.BlockSpec(memory_space=pltpu.VMEM)
    smem = pl.BlockSpec(memory_space=pltpu.SMEM)
    params = pltpu.CompilerParams(vmem_limit_bytes=VMEM_LIMIT)
    column = jnp.concatenate(
        [positions.reshape(3, slots), species.reshape(1, slots).astype(F32)], axis=0
    )
    sems = [pltpu.SemaphoreType.DMA((9,)), pltpu.SemaphoreType.DMA((9,))]
    table = pl.pallas_call(
        spread_kernel,
        out_shape=jax.ShapeDtypeStruct((36, width), F32),
        in_specs=[smem, vmem],
        out_specs=vmem,
        scratch_shapes=[pltpu.VMEM((4, width), F32), pltpu.VMEM((9, 4, width), F32)] + sems,
        compiler_params=pltpu.CompilerParams(
            vmem_limit_bytes=VMEM_LIMIT, collective_id=0, has_side_effects=True
        ),
    )(counts, column)

    chunks = neigh // ROWS
    span = ROWS * LANES
    latent = mixer_weight.shape[0]
    whole = lambda array: pl.BlockSpec(array.shape, lambda b: (0,) * array.ndim)
    by_block = lambda rows: pl.BlockSpec((rows, LANES), lambda b: (0, b))
    operands = [
        embed_weight.T,
        mixer_weight,
        tensor_weight,
        update_weight,
        output_weight.reshape(latent, 1),
    ]
    energy, partials = pl.pallas_call(
        layer_kernel,
        grid=(slots // LANES,),
        out_shape=(
            jax.ShapeDtypeStruct((1, slots), F32),
            jax.ShapeDtypeStruct((27, width), F32),
        ),
        in_specs=[smem, smem, whole(table), by_block(4), by_block(neigh)]
        + [whole(array) for array in operands],
        out_specs=(by_block(1), pl.BlockSpec((27, width), lambda b: (0, 0))),
        scratch_shapes=[
            pltpu.VMEM((9, neigh, LANES), F32),
            pltpu.VMEM((5, neigh, LANES), F32),
            pltpu.VMEM((chunks, 8, span), F32),
            pltpu.VMEM((chunks, latent, span), BF16),
            pltpu.VMEM((chunks, latent, span), BF16),
            pltpu.VMEM((chunks, latent, span), BF16),
            pltpu.VMEM((chunks, latent, span), BF16),
            pltpu.VMEM((chunks, 32, span), F32),
            pltpu.VMEM((chunks, latent, span), BF16),
            pltpu.VMEM((chunks, 16, span), BF16),
            pltpu.VMEM((4, 16, LANES), F32),
            pltpu.VMEM((4, 16, LANES), F32),
            pltpu.VMEM((STRIDES, 27, LANES), F32),
            pltpu.VMEM(embed_weight.shape, BF16),
            pltpu.VMEM(mixer_weight.shape[::-1], BF16),
            pltpu.VMEM(tensor_weight.shape[::-1], BF16),
            pltpu.VMEM(update_weight.shape[::-1], BF16),
        ],
        compiler_params=params,
    )(counts, pair_scale, table, column, neighbours.reshape(neigh, slots), *operands)

    forces = pl.pallas_call(
        fold_kernel,
        out_shape=jax.ShapeDtypeStruct((3, slots), F32),
        in_specs=[smem, vmem],
        out_specs=vmem,
        scratch_shapes=[pltpu.VMEM((9, 4, width), F32), pltpu.VMEM((9, 4, width), F32)] + sems,
        compiler_params=pltpu.CompilerParams(
            vmem_limit_bytes=VMEM_LIMIT, collective_id=1, has_side_effects=True
        ),
    )(counts, partials)
    return energy.reshape(1, 1, slots), forces.reshape(3, 1, 1, slots)


def solution(mesh):
    return jax.shard_map(
        body,
        mesh=mesh,
        in_specs=(
            P(None, "gx", "gy", None),
            P("gx", "gy", None),
            P("gx", "gy"),
            P(None, "gx", "gy", None),
            P(),
            P(),
            P(),
            P(),
            P(),
            P(),
        ),
        out_specs=(P("gx", "gy", None), P(None, "gx", "gy", None)),
        check_vma=False,
    )
```
